256 devices in a mesh: ckpt: 16 (over y, z_hi), corpus: 16 (over x, z_lo, core).
Axes of the slice: x: 4, y: 4, z: 8 (z_hi: 4, z_lo: 2; z = z_hi * 2 + z_lo), core: 2. Of those that a mesh axis runs over, the one named last changes fastest.
Arguments:
- activations: bfloat16 [16, 2048, 4096], P('ckpt', 'corpus'), may hold values from -6 to 6
- cotangents: bfloat16 [16, 2048, 4096], P('ckpt', 'corpus'), may hold values from -6 to 6
- adapter_down: bfloat16 [16, 4096, 64], P('ckpt'), may hold values from -0.09375 to 0.09375
- projection: bfloat16 [4096, 64], replicated, may hold values from -0.09375 to 0.09375
- learning_rates: int32 [16], P('ckpt'), may hold values from 1 to 8
- gradient_store: bfloat16 [16, 16384, 4096], P('ckpt', 'corpus'), may hold values from -0.09375 to 0.09375
- example_slot: int32 [16, 16, 1024], P('ckpt', 'corpus'), may hold values from 0 to 1023, each once within a row
- query_of_token: int32 [16, 128], replicated, may hold values from 0 to 15, never falling along the last dimension, each value on 1 to 12 neighbouring positions
Outputs:
- influence: float32 [256, 16384], P('ckpt', 'corpus')
The draws below stay inside these ranges and needn't reach their ends.
Inputs may be any that keep to these rules, and one draw needn't show every extreme that they name: Each row of example_slot is a permutation of 0 to 1023. Each row of query_of_token never falls and gives every query of the shard 1 to 12 tokens; some query has exactly 12.
All inputs are finite; a program needn't handle non-finite values.
Results may differ from the reference program's by a relative error of at most 0.005.
Values may be sent and summed in bfloat16 or wider, within the bound.
No kernel may reach another device: no remote copies, remote signals or barrier semaphores. Data moves between devices by JAX's collectives and lax.ppermute only.
A program may use at most 64 MiB of HBM per device.

```python
import math
import jax
import jax.numpy as jnp
import numpy as np

D = 4096
R = 64
K = 64
QUERIES = 256
TOK_DEV = 128
ROWS_DEV = 1024
CKPTS = 16
SHARDS = 16
QRY_DEV = 16
MOST = 12
TOKENS = 2048
EXAMPLES = 16384


def touch_ends(values, rng, least, largest):
    dims = values.shape
    index_at = [jax.random.randint(jax.random.fold_in(rng, axis), (), 0, dims[axis]) for axis in range(len(dims))]
    values = values.at[tuple(index_at)].set(least)
    longest = dims.index(max(dims))
    index_at[longest] = (index_at[longest] + 1) % dims[longest]
    return values.at[tuple(index_at)].set(largest)


def shard_levels(own_key, shape, split, least, high):
    def one(position, parts):
        heights = jax.random.uniform(jax.random.fold_in(jax.random.fold_in(own_key, 6), position), (parts,), jnp.float32, least / len(split), high / len(split))
        return jnp.repeat(jnp.exp(heights), shape[position] // parts).reshape((-1,) + (1,) * (len(shape) - position - 1))

    level = one(*split[0])
    for cut in split[1:]:
        level = level * one(*cut)
    return level


def profile(amount, total, most, slope):
    portions = [(1 << 20) // math.isqrt(standing ** slope) + 1 for standing in range(2, amount + 1)]
    surplus, holding = total - most - (amount - 1), [1] * (amount - 1)
    while surplus > 0:
        candidates = [i for i in range(amount - 1) if holding[i] < most]
        pool, left = sum([portions[i] for i in candidates]), surplus
        for i in candidates:
            extra = min(most - holding[i], max(1, left * portions[i] // pool), surplus)
            holding[i] = holding[i] + extra
            surplus = surplus - extra
    return np.array([most] + holding)


def uneven(own_key, amount, total, bound, lean):
    if amount == 2:
        one = jax.random.randint(own_key, (), max(1, total - bound), min(bound, total - 1) + 1)
        return jnp.stack([one, total - one])
    tallies = jnp.asarray(profile(amount, total, bound, lean), jnp.int32)
    pairs = (amount - 1) // 2
    donor, receiver = tallies[1:1 + 2 * pairs:2], tallies[2:2 + 2 * pairs:2]
    room = jnp.minimum(donor - 1, bound - receiver)
    shifted = jax.random.randint(jax.random.fold_in(own_key, 1), (pairs,), 0, 1 << 20) % (room + 1)
    tallies = tallies.at[1:1 + 2 * pairs:2].set(donor - shifted).at[2:2 + 2 * pairs:2].set(receiver + shifted)
    return tallies[jax.random.permutation(jax.random.fold_in(own_key, 2), amount)]


def centred(stream_key, dims, scale, bound, cuts=(), kind=jnp.bfloat16):
    factor_of = shard_levels(stream_key, dims, cuts, -0.22, 0.18) if cuts else 1.0
    values = jax.random.normal(stream_key, dims, jnp.float32) * scale * factor_of
    return jnp.minimum(jnp.maximum(values, -bound), bound).astype(kind)


def setup_inputs(seed: int = 0) -> dict:
    key_of = jax.random.split(jax.random.key(seed), 9)
    return {
        "activations": centred(key_of[0], (CKPTS, TOKENS, D), 1.0, 6.0, ((0, 16), (1, 16))),
        "cotangents": centred(key_of[1], (CKPTS, TOKENS, D), 1.0, 6.0, ((0, 16), (1, 16))),
        "adapter_down": centred(key_of[2], (CKPTS, D, R), D ** -0.5, 0.09375, ((0, 16),)),
        "projection": centred(key_of[3], (D, K), D ** -0.5, 0.09375),
        "learning_rates": touch_ends(jax.random.randint(key_of[4], (CKPTS,), 1, 9), jax.random.fold_in(key_of[4], 1), 1, 8).astype(jnp.int32),
        "gradient_store": centred(key_of[5], (CKPTS, EXAMPLES, R * K), (R * K) ** -0.5, 0.09375, ((0, 16), (1, 16))),
        "example_slot": jax.vmap(lambda own: jax.random.permutation(own, ROWS_DEV))(jax.random.split(key_of[6], CKPTS * SHARDS)).reshape((CKPTS, SHARDS, ROWS_DEV)).astype(jnp.int32),
        "query_of_token": jax.vmap(lambda own: jnp.searchsorted(jnp.cumsum(uneven(own, QRY_DEV, TOK_DEV, MOST, 2)), jnp.arange(TOK_DEV), side="right"))(jax.random.split(key_of[7], SHARDS)).reshape((SHARDS, TOK_DEV)).astype(jnp.int32),
    }


def query_gradients(member_ids, low_in, low_out, per_shard):
    member = (member_ids[:, :, None] == jnp.arange(per_shard, dtype=jnp.int32)[None, None, :]).astype(jnp.float32)
    weighted = jnp.einsum('btq,btr->btqr', member, low_in.astype(jnp.float32))
    gradients = jnp.einsum('btqr,btk->bqrk', weighted, low_out.astype(jnp.float32))
    blocks, queries, rank_width, out_width = gradients.shape
    return gradients.reshape(blocks * queries, rank_width * out_width).astype(jnp.bfloat16)


def reference(activations, cotangents, adapter_down, projection, learning_rates, gradient_store, example_slot, query_of_token):
    total = jnp.zeros((QUERIES, EXAMPLES), jnp.float32)
    for index in range(CKPTS):
        low_in = jnp.dot(activations[index], adapter_down[index], preferred_element_type=jnp.float32).astype(jnp.bfloat16)
        low_out = jnp.dot(cotangents[index], projection, preferred_element_type=jnp.float32).astype(jnp.bfloat16)
        grads = query_gradients(query_of_token, low_in.reshape(SHARDS, TOK_DEV, R), low_out.reshape(SHARDS, TOK_DEV, K), QRY_DEV)
        scores = jax.lax.dot_general(grads, gradient_store[index], (((1,), (1,)), ((), ())), preferred_element_type=jnp.float32)
        example_ids = (jnp.arange(SHARDS, dtype=jnp.int32)[:, None] * ROWS_DEV + example_slot[index]).reshape(-1).astype(jnp.int32)
        placed = jnp.zeros_like(scores).at[:, example_ids].set(scores)
        total = total + learning_rates[index].astype(jnp.float32) * placed
    return total / CKPTS
```

```python
import functools

import jax
import jax.numpy as jnp
from jax import lax
from jax.experimental import pallas as pl
from jax.experimental.pallas import tpu as pltpu
from jax.sharding import PartitionSpec as P

BF16 = jnp.bfloat16
F32 = jnp.float32
NT = (((1,), (1,)), ((), ()))
VMEM = pl.BlockSpec(memory_space=pltpu.VMEM)
SMEM = pl.BlockSpec(memory_space=pltpu.SMEM)
MIB = 1 << 20
SIDE = 4


def factors_kernel(act_ref, cot_ref, down_ref, proj_ref, out_ref, both):
    rank = down_ref.shape[1]
    low_in = jnp.dot(act_ref[...], down_ref[...], preferred_element_type=F32)
    low_out = jnp.dot(cot_ref[...], proj_ref[...], preferred_element_type=F32)
    both[...] = jnp.concatenate([low_in, low_out], axis=1).T
    half = rank // 2
    out_ref[0:half, :] = both[pl.ds(0, half, 2), :].astype(BF16)
    out_ref[half:rank, :] = both[pl.ds(1, half, 2), :].astype(BF16)
    out_ref[rank:, :] = both[rank:, :].astype(BF16)


def factors(act, cot, down, proj):
    tokens, rank, width = act.shape[0], down.shape[1], proj.shape[1]
    return pl.pallas_call(
        factors_kernel,
        out_shape=jax.ShapeDtypeStruct((rank + width, tokens), BF16),
        in_specs=[VMEM] * 4,
        out_specs=VMEM,
        scratch_shapes=[pltpu.VMEM((rank + width, tokens), F32)],
        compiler_params=pltpu.CompilerParams(vmem_limit_bytes=16 * MIB),
        name="factors",
    )(act, cot, down, proj)


def scores_kernel(
    rate_ref, slot_ref, ids_ref, mine_ref, other_ref, store_ref, o0, o1, o2, o3, grads, placed
):
    corpus, ckpt = lax.axis_index("corpus"), lax.axis_index("ckpt")
    x, zlo, core = corpus // 4, (corpus // 2) % 2, corpus % 2
    y, zhi = ckpt // SIDE, ckpt % SIDE
    pieces, depth, tokens = mine_ref.shape
    half = depth // 4
    rows = ids_ref.shape[0]

    def piece(k, ref, flip):
        shard = ((x + SIDE - k // 2) % SIDE) * 4 + (zlo + k % 2) % 2 * 2 + (core + flip) % 2
        at = ((shard // SIDE + SIDE - y) % SIDE) * SIDE + (shard % SIDE + SIDE - zhi) % SIDE
        base = pl.multiple_of(at * rows, rows)
        member = ids_ref[pl.ds(shard, 1), :] == lax.broadcasted_iota(
            jnp.int32, (rows, tokens), 0
        )
        block = ref[k]
        low = block[: 2 * half].astype(F32)
        weights = [
            jnp.where(member[None], low[h * half : (h + 1) * half, None, :], 0.0)
            .astype(BF16)
            .reshape(half * rows, tokens)
            for h in range(2)
        ]
        left = jnp.concatenate(weights, axis=1)
        low_out = block[2 * half :]
        blank = jnp.zeros_like(low_out)
        right = jnp.concatenate(
            [
                jnp.concatenate([low_out, blank], axis=1),
                jnp.concatenate([blank, low_out], axis=1),
            ],
            axis=0,
        )
        product = lax.dot_general(left, right, NT, preferred_element_type=F32).astype(BF16)
        lanes = product.shape[1]
        for p in range(half):
            grads[pl.ds(base, rows), p * lanes : (p + 1) * lanes] = product[
                p * rows : (p + 1) * rows
            ]

    for ref, flip in ((mine_ref, 0), (other_ref, 1)):
        @pl.loop(0, pieces)
        def _(k):
            piece(k, ref, flip)

    examples = store_ref.shape[0]
    chunk = 256
    weight = rate_ref[0].astype(F32) * (1.0 / lax.axis_size("ckpt"))

    @pl.loop(0, examples // chunk)
    def _(c):
        at = pl.multiple_of(c * chunk, chunk)
        part = lax.dot_general(
            grads[...], store_ref[pl.ds(at, chunk), :], NT, preferred_element_type=F32
        )
        placed[:, pl.ds(at, chunk)] = (part * weight).astype(BF16)

    slot = slot_ref[...]
    for c in range(examples // chunk):
        column = lax.broadcasted_iota(jnp.int32, (chunk, examples), 0) + c * chunk
        choose = jnp.where(column == slot, 1.0, 0.0).astype(BF16)
        moved = lax.dot_general(placed[...], choose, NT, preferred_element_type=F32).astype(BF16)
        quarter = moved.shape[0] // SIDE
        for k, out in enumerate((o0, o1, o2, o3)):
            out[:, c * chunk : (c + 1) * chunk] = moved[k * quarter : (k + 1) * quarter]


def scores(rate, slot, ids, mine, other, store):
    shards, per_shard = ids.shape[0], 16
    queries, examples = shards * per_shard, store.shape[0]
    return pl.pallas_call(
        scores_kernel,
        out_shape=[jax.ShapeDtypeStruct((queries // SIDE, examples), BF16)] * SIDE,
        in_specs=[SMEM] + [VMEM] * 5,
        out_specs=[VMEM] * SIDE,
        scratch_shapes=[
            pltpu.VMEM((queries, store.shape[1]), BF16),
            pltpu.VMEM((queries, examples), BF16),
        ],
        compiler_params=pltpu.CompilerParams(vmem_limit_bytes=32 * MIB),
        name="scores",
    )(rate, slot, ids, mine, other, store)


def add_kernel(a, b, c, d, *outs):
    total = (a[...].astype(F32) + b[...].astype(F32)) + (c[...].astype(F32) + d[...].astype(F32))
    rows = outs[0].shape[0]
    for k, out in enumerate(outs):
        out[...] = total[k * rows : (k + 1) * rows].astype(out.dtype)


def add(parts, outs, dtype):
    rows, columns = parts[0].shape
    return pl.pallas_call(
        add_kernel,
        out_shape=[jax.ShapeDtypeStruct((rows // outs, columns), dtype)] * outs,
        in_specs=[VMEM] * SIDE,
        out_specs=[VMEM] * outs,
        name="add",
    )(*parts)


def along(parts, axis, shift):
    n = lax.axis_size(axis)
    return [parts[0]] + [
        lax.ppermute(parts[k], axis, [(i, shift(i, k)) for i in range(n)]) for k in (2, 1, 3)
    ]


def shards(
    activations,
    cotangents,
    adapter_down,
    projection,
    learning_rates,
    gradient_store,
    example_slot,
    query_of_token,
):
    own = factors(activations[0], cotangents[0], adapter_down[0], projection)
    near = lax.ppermute(own, "corpus", [(i, i ^ 2) for i in range(16)])
    pair = jnp.stack([own, near])
    line = [pair] + [
        lax.ppermute(pair, "corpus", [(i, (i + 4 * k) % 16) for i in range(16)]) for k in (1, 2, 3)
    ]
    mine = jnp.concatenate(line)
    other = lax.ppermute(mine, "corpus", [(i, i ^ 1) for i in range(16)])
    store = pltpu.with_memory_space_constraint(gradient_store[0], pltpu.VMEM)
    blocks = scores(learning_rates, example_slot[0], query_of_token, mine, other, store)
    rows = along(blocks, "ckpt", lambda i, k: (i + 4 * k) % 16)
    blocks = add(rows, SIDE, BF16)
    cells = along(blocks, "ckpt", lambda i, k: i // 4 * 4 + (i + k) % 4)
    return add(cells, 1, F32)[0]


def solution(mesh):
    return jax.shard_map(
        shards,
        mesh=mesh,
        in_specs=(
            P("ckpt", "corpus", None),
            P("ckpt", "corpus", None),
            P("ckpt", None, None),
            P(),
            P("ckpt"),
            P("ckpt", "corpus", None),
            P("ckpt", "corpus", None),
            P(),
        ),
        out_specs=P("ckpt", "corpus"),
        check_vma=False,
    )
```

```python
import jax
import jax.numpy as jnp
from jax import lax
from jax.experimental import pallas as pl
from jax.experimental.pallas import tpu as pltpu
from jax.sharding import PartitionSpec as P

BF16 = jnp.bfloat16
F32 = jnp.float32
NT = (((1,), (1,)), ((), ()))
VMEM = pl.BlockSpec(memory_space=pltpu.VMEM)
SMEM = pl.BlockSpec(memory_space=pltpu.SMEM)
HBM = pl.BlockSpec(memory_space=pltpu.HBM)
MIB = 1 << 20
ANY = pl.BlockSpec(memory_space=pl.ANY)
CUTS = 4
PARTS = 2
ROWS = 16
SIDE = 4
ORDER = (2, 1, 3)
STEPS = (0, 1, 3, 2)


def factors_kernel(act_hbm, cot_hbm, down_hbm, proj_hbm, out_ref, act, cot, down, proj, both, sems):
    pairs = ((act_hbm, act), (down_hbm, down), (cot_hbm, cot), (proj_hbm, proj))
    width = act.shape[1] // CUTS
    copies = [
        [
            pltpu.make_async_copy(
                src.at[:, pl.ds(c * width, width)], dst.at[:, pl.ds(c * width, width)], sems.at[k, c]
            )
            for k, (src, dst) in enumerate(pairs)
        ]
        for c in range(CUTS)
    ]
    for group in copies:
        for copy in group:
            copy.start()
    rank = down.shape[0]
    low_in, low_out = 0.0, 0.0
    for c, group in enumerate(copies):
        for copy in group:
            copy.wait()
        at = slice(c * width, (c + 1) * width)
        low_in += lax.dot_general(down[:, at], act[:, at], NT, preferred_element_type=F32)
        low_out += lax.dot_general(proj[:, at], cot[:, at], NT, preferred_element_type=F32)
    both[...] = low_in
    half = rank // 2
    out_ref[0:half, :] = both[pl.ds(0, half, 2), :].astype(BF16)
    out_ref[half:rank, :] = both[pl.ds(1, half, 2), :].astype(BF16)
    out_ref[rank:, :] = low_out.astype(BF16)


def factors(act, cot, down, proj):
    tokens, rank, width = act.shape[0], down.shape[0], proj.shape[0]
    arrays = [pltpu.with_memory_space_constraint(x, pltpu.HBM) for x in (act, cot, down, proj)]
    return pl.pallas_call(
        factors_kernel,
        out_shape=jax.ShapeDtypeStruct((rank + width, tokens), BF16),
        in_specs=[HBM] * 4,
        out_specs=VMEM,
        scratch_shapes=[pltpu.VMEM(x.shape, BF16) for x in arrays]
        + [pltpu.VMEM((rank, tokens), F32), pltpu.SemaphoreType.DMA((4, CUTS))],
        compiler_params=pltpu.CompilerParams(vmem_limit_bytes=8 * MIB),
        name="factors",
    )(*arrays)


def build(ids_ref, shard, block, rows):
    tokens = block.shape[1]
    half = block.shape[0] // 4
    member = ids_ref[pl.ds(shard, 1), :] == lax.broadcasted_iota(jnp.int32, (rows, tokens), 0)
    low = block[: 2 * half].astype(F32)
    weights = [
        jnp.where(member[None], low[h * half : (h + 1) * half, None, :], 0.0)
        .astype(BF16)
        .reshape(half * rows, tokens)
        for h in range(2)
    ]
    left = jnp.concatenate(weights, axis=1)
    low_out = block[2 * half :]
    blank = jnp.zeros_like(low_out)
    right = jnp.concatenate(
        [
            jnp.concatenate([low_out, blank], axis=1),
            jnp.concatenate([blank, low_out], axis=1),
        ],
        axis=0,
    )
    return lax.dot_general(left, right, NT, preferred_element_type=F32).astype(BF16)


def shard_of(k, flip):
    corpus = lax.axis_index("corpus")
    x, zlo, core = corpus // 4, (corpus // 2) % 2, corpus % 2
    return ((x + SIDE - STEPS[k // 2]) % SIDE) * 4 + (zlo + k % 2) % 2 * 2 + (core + flip) % 2


def row_of(shard, rows):
    ckpt = lax.axis_index("ckpt")
    y, zhi = ckpt // SIDE, ckpt % SIDE
    at = ((shard // SIDE + SIDE - y) % SIDE) * SIDE + (shard % SIDE + SIDE - zhi) % SIDE
    return pl.multiple_of(at * rows, rows)


def choose_kernel(
    rate_ref, slot_hbm, ids_hbm, after_hbm, out_ref, weight_ref, ids_ref, slot_ref, sems
):
    load = pltpu.make_async_copy(slot_hbm, slot_ref, sems.at[0])
    ids_load = pltpu.make_async_copy(ids_hbm, ids_ref, sems.at[1])
    load.start()
    ids_load.start()
    weight_ref[...] = jnp.full(
        weight_ref.shape, rate_ref[0].astype(F32) * (1.0 / lax.axis_size("ckpt")), F32
    )
    load.wait()
    examples = slot_ref.shape[1]
    slot = slot_ref[...]
    step = 128
    for c in range(examples // step):
        column = lax.broadcasted_iota(jnp.int32, (step, examples), 0) + c * step
        out_ref[c * step : (c + 1) * step, :] = jnp.where(column == slot, 1.0, 0.0).astype(BF16)
    ids_load.wait()


def choose(rate, slot, ids, after):
    examples = slot.shape[1]
    return pl.pallas_call(
        choose_kernel,
        out_shape=[
            jax.ShapeDtypeStruct((examples, examples), BF16),
            jax.ShapeDtypeStruct((8, 128), F32),
            jax.ShapeDtypeStruct(ids.shape, ids.dtype),
        ],
        in_specs=[SMEM, HBM, HBM, ANY],
        out_specs=[VMEM] * 3,
        scratch_shapes=[pltpu.VMEM(slot.shape, jnp.int32), pltpu.SemaphoreType.DMA((2,))],
        compiler_params=pltpu.CompilerParams(vmem_limit_bytes=4 * MIB),
        cost_estimate=pl.CostEstimate(flops=10**10, bytes_accessed=2 * MIB, transcendentals=0),
        name="choose",
    )(rate, *(pltpu.with_memory_space_constraint(x, pltpu.HBM) for x in (slot, ids)), after)


def near_kernel(ids_ref, mine_ref, out_ref):
    rows = out_ref.shape[0] // mine_ref.shape[0]
    for k in range(mine_ref.shape[0]):
        product = build(ids_ref, shard_of(k, 0), mine_ref[k], rows)
        lanes = product.shape[1]
        for p in range(product.shape[0] // rows):
            out_ref[k * rows : (k + 1) * rows, p * lanes : (p + 1) * lanes] = product[
                p * rows : (p + 1) * rows
            ]


def near_grads(ids, mine, width):
    queries = mine.shape[0] * ROWS
    return pl.pallas_call(
        near_kernel,
        out_shape=jax.ShapeDtypeStruct((queries, width), BF16),
        in_specs=[VMEM, VMEM],
        out_specs=VMEM,
        compiler_params=pltpu.CompilerParams(vmem_limit_bytes=4 * MIB),
        cost_estimate=pl.CostEstimate(flops=10**9, bytes_accessed=2 * MIB, transcendentals=0),
        name="near_grads",
    )(ids, mine)


def scores_kernel(
    ids_ref, near_ref, other_ref, choose_ref, weight_ref, store_ref, o0, o1, o2, o3,
    grads, placed,
):
    examples = store_ref.shape[0]
    pieces = other_ref.shape[0]
    rows = ROWS
    for k in range(pieces):
        grads[pl.ds(row_of(shard_of(k, 0), rows), rows), :] = near_ref[k * rows : (k + 1) * rows, :]
    for k in range(pieces):
        shard = shard_of(k, 1)
        product = build(ids_ref, shard, other_ref[k], rows)
        base = row_of(shard, rows)
        lanes = product.shape[1]
        for p in range(product.shape[0] // rows):
            grads[pl.ds(base, rows), p * lanes : (p + 1) * lanes] = product[
                p * rows : (p + 1) * rows
            ]

    weight = weight_ref[0:1, 0:1]
    chunk = examples // PARTS
    for c in range(PARTS):
        at = slice(c * chunk, (c + 1) * chunk)
        part = lax.dot_general(grads[...], store_ref[at, :], NT, preferred_element_type=F32)
        placed[:, at] = (part * weight).astype(BF16)

    moved = lax.dot_general(placed[...], choose_ref[...], NT, preferred_element_type=F32)
    moved = moved.astype(BF16)
    quarter = moved.shape[0] // SIDE
    for k, out in enumerate((o0, o1, o2, o3)):
        out[...] = moved[k * quarter : (k + 1) * quarter]


def scores(ids, near, other, chosen, weight, store):
    queries, examples = ids.shape[0] * ROWS, store.shape[0]
    return pl.pallas_call(
        scores_kernel,
        out_shape=[jax.ShapeDtypeStruct((queries // SIDE, examples), BF16)] * SIDE,
        in_specs=[VMEM] * 6,
        out_specs=[VMEM] * SIDE,
        scratch_shapes=[
            pltpu.VMEM((queries, store.shape[1]), BF16),
            pltpu.VMEM((queries, examples), BF16),
        ],
        compiler_params=pltpu.CompilerParams(vmem_limit_bytes=8 * MIB),
        name="scores",
    )(ids, near, other, chosen, weight, store)


def add_kernel(a, b, c, d, *outs):
    total = (a[...].astype(F32) + b[...].astype(F32)) + (c[...].astype(F32) + d[...].astype(F32))
    rows = outs[0].shape[0]
    for k, out in enumerate(outs):
        out[...] = total[k * rows : (k + 1) * rows].astype(out.dtype)


def add(parts, outs, dtype):
    rows, columns = parts[0].shape
    return pl.pallas_call(
        add_kernel,
        out_shape=[jax.ShapeDtypeStruct((rows // outs, columns), dtype)] * outs,
        in_specs=[VMEM] * SIDE,
        out_specs=[VMEM] * outs,
        compiler_params=pltpu.CompilerParams(vmem_limit_bytes=4 * MIB),
        name="add",
    )(*parts)


def along(parts, axis, shift, order=ORDER):
    n = lax.axis_size(axis)
    return [parts[0]] + [
        lax.ppermute(parts[k], axis, [(i, shift(i, k)) for i in range(n)]) for k in order
    ]


def shards(
    activations,
    cotangents,
    adapter_down,
    projection,
    learning_rates,
    gradient_store,
    example_slot,
    query_of_token,
):
    own = factors(activations[0], cotangents[0], adapter_down[0].T, projection.T)
    near = lax.ppermute(own, "corpus", [(i, i ^ 2) for i in range(16)])
    chosen, weight, ids = choose(learning_rates, example_slot[0], query_of_token, own)
    pair = jnp.stack([own, near])
    mine = jnp.concatenate(
        along([pair] * SIDE, "corpus", lambda i, k: (i + 4 * k) % 16, STEPS[1:])
    )
    mine, chosen = lax.optimization_barrier((mine, chosen))
    other = lax.ppermute(mine, "corpus", [(i, i ^ 1) for i in range(16)])
    store = gradient_store[0]
    near_part = near_grads(ids, mine, store.shape[1])
    blocks = scores(ids, near_part, other, chosen, weight, store)
    rows = along(blocks, "ckpt", lambda i, k: (i + 4 * k) % 16)
    blocks = add(rows, SIDE, BF16)
    cells = along(blocks, "ckpt", lambda i, k: i // 4 * 4 + (i + k) % 4)
    return add(cells, 1, F32)[0]


def solution(mesh):
    return jax.shard_map(
        shards,
        mesh=mesh,
        in_specs=(
            P("ckpt", "corpus", None),
            P("ckpt", "corpus", None),
            P("ckpt", None, None),
            P(),
            P("ckpt"),
            P("ckpt", "corpus", None),
            P("ckpt", "corpus", None),
            P(),
        ),
        out_specs=P("ckpt", "corpus"),
        check_vma=False,
    )
```

```python
import functools

import jax
import jax.numpy as jnp
from jax import lax
from jax.experimental import pallas as pl
from jax.experimental.pallas import tpu as pltpu
from jax.sharding import PartitionSpec as P

BF16 = jnp.bfloat16
F32 = jnp.float32
NT = (((1,), (1,)), ((), ()))
VMEM = pl.BlockSpec(memory_space=pltpu.VMEM)
SMEM = pl.BlockSpec(memory_space=pltpu.SMEM)
HBM = pl.BlockSpec(memory_space=pltpu.HBM)
MIB = 1 << 20
ANY = pl.BlockSpec(memory_space=pl.ANY)
CUTS = 4
PARTS = 2
ROWS = 16
SIDE = 4
ORDER = (2, 1, 3)
STEPS = (0, 1, 3, 2)


def factors_kernel(act_hbm, cot_hbm, down_hbm, proj_hbm, out_ref, act, cot, down, proj, both, sems):
    pairs = ((act_hbm, act), (down_hbm, down), (cot_hbm, cot), (proj_hbm, proj))
    width = act.shape[1] // CUTS
    copies = [
        [
            pltpu.make_async_copy(
                src.at[:, pl.ds(c * width, width)], dst.at[:, pl.ds(c * width, width)], sems.at[k, c]
            )
            for k, (src, dst) in enumerate(pairs)
        ]
        for c in range(CUTS)
    ]
    for group in copies:
        for copy in group:
            copy.start()
    rank = down.shape[0]
    low_in, low_out = 0.0, 0.0
    for c, group in enumerate(copies):
        for copy in group:
            copy.wait()
        at = slice(c * width, (c + 1) * width)
        low_in += lax.dot_general(down[:, at], act[:, at], NT, preferred_element_type=F32)
        low_out += lax.dot_general(proj[:, at], cot[:, at], NT, preferred_element_type=F32)
    both[...] = low_in
    half = rank // 2
    out_ref[0:half, :] = both[pl.ds(0, half, 2), :].astype(BF16)
    out_ref[half:rank, :] = both[pl.ds(1, half, 2), :].astype(BF16)
    out_ref[rank:, :] = low_out.astype(BF16)


def factors(act, cot, down, proj):
    tokens, rank, width = act.shape[0], down.shape[0], proj.shape[0]
    arrays = [pltpu.with_memory_space_constraint(x, pltpu.HBM) for x in (act, cot, down, proj)]
    return pl.pallas_call(
        factors_kernel,
        out_shape=jax.ShapeDtypeStruct((rank + width, tokens), BF16),
        in_specs=[HBM] * 4,
        out_specs=VMEM,
        scratch_shapes=[pltpu.VMEM(x.shape, BF16) for x in arrays]
        + [pltpu.VMEM((rank, tokens), F32), pltpu.SemaphoreType.DMA((4, CUTS))],
        compiler_params=pltpu.CompilerParams(vmem_limit_bytes=8 * MIB),
        name="factors",
    )(*arrays)


def build(ids_ref, shard, block, rows):
    tokens = block.shape[1]
    half = block.shape[0] // 4
    member = ids_ref[pl.ds(shard, 1), :] == lax.broadcasted_iota(jnp.int32, (rows, tokens), 0)
    low = block[: 2 * half].astype(F32)
    weights = [
        jnp.where(member[None], low[h * half : (h + 1) * half, None, :], 0.0)
        .astype(BF16)
        .reshape(half * rows, tokens)
        for h in range(2)
    ]
    left = jnp.concatenate(weights, axis=1)
    low_out = block[2 * half :]
    blank = jnp.zeros_like(low_out)
    right = jnp.concatenate(
        [
            jnp.concatenate([low_out, blank], axis=1),
            jnp.concatenate([blank, low_out], axis=1),
        ],
        axis=0,
    )
    return lax.dot_general(left, right, NT, preferred_element_type=F32).astype(BF16)


def shard_of(k, flip):
    corpus = lax.axis_index("corpus")
    x, zlo, core = corpus // 4, (corpus // 2) % 2, corpus % 2
    return (x ^ STEPS[k // 2]) * 4 + (zlo ^ (k % 2)) * 2 + (core ^ flip)


def row_of(shard, rows):
    ckpt = lax.axis_index("ckpt")
    y, zhi = ckpt // SIDE, ckpt % SIDE
    at = ((shard // SIDE) ^ y) * SIDE + ((shard % SIDE) ^ zhi)
    return pl.multiple_of(at * rows, rows)


def choose_kernel(
    rate_ref, slot_hbm, ids_hbm, after_hbm, out_ref, weight_ref, ids_ref, slot_ref, sems
):
    load = pltpu.make_async_copy(slot_hbm, slot_ref, sems.at[0])
    ids_load = pltpu.make_async_copy(ids_hbm, ids_ref, sems.at[1])
    load.start()
    ids_load.start()
    weight_ref[...] = jnp.full(
        weight_ref.shape, rate_ref[0].astype(F32) * (1.0 / lax.axis_size("ckpt")), F32
    )
    load.wait()
    examples = slot_ref.shape[1]
    slot = slot_ref[...]
    step = 128
    for c in range(examples // step):
        column = lax.broadcasted_iota(jnp.int32, (step, examples), 0) + c * step
        out_ref[c * step : (c + 1) * step, :] = jnp.where(column == slot, 1.0, 0.0).astype(BF16)
    ids_load.wait()


def choose(rate, slot, ids, after):
    examples = slot.shape[1]
    return pl.pallas_call(
        choose_kernel,
        out_shape=[
            jax.ShapeDtypeStruct((examples, examples), BF16),
            jax.ShapeDtypeStruct((8, 128), F32),
            jax.ShapeDtypeStruct(ids.shape, ids.dtype),
        ],
        in_specs=[SMEM, HBM, HBM, ANY],
        out_specs=[VMEM] * 3,
        scratch_shapes=[pltpu.VMEM(slot.shape, jnp.int32), pltpu.SemaphoreType.DMA((2,))],
        compiler_params=pltpu.CompilerParams(vmem_limit_bytes=4 * MIB),
        cost_estimate=pl.CostEstimate(flops=10**10, bytes_accessed=2 * MIB, transcendentals=0),
        name="choose",
    )(rate, *(pltpu.with_memory_space_constraint(x, pltpu.HBM) for x in (slot, ids)), after)


def near_kernel(ids_ref, mine_ref, out_ref):
    rows = out_ref.shape[0] // mine_ref.shape[0]
    for k in range(mine_ref.shape[0]):
        product = build(ids_ref, shard_of(k, 0), mine_ref[k], rows)
        lanes = product.shape[1]
        for p in range(product.shape[0] // rows):
            out_ref[k * rows : (k + 1) * rows, p * lanes : (p + 1) * lanes] = product[
                p * rows : (p + 1) * rows
            ]


def near_grads(ids, mine, width):
    queries = mine.shape[0] * ROWS
    return pl.pallas_call(
        near_kernel,
        out_shape=jax.ShapeDtypeStruct((queries, width), BF16),
        in_specs=[VMEM, VMEM],
        out_specs=VMEM,
        compiler_params=pltpu.CompilerParams(vmem_limit_bytes=4 * MIB),
        cost_estimate=pl.CostEstimate(flops=10**9, bytes_accessed=2 * MIB, transcendentals=0),
        name="near_grads",
    )(ids, mine)


def scores_kernel(
    ids_ref, near_ref, other_ref, choose_ref, weight_ref, store_ref,
    home, cross, a1, a3, b1, b3, grads, placed,
):
    examples = store_ref.shape[0]
    pieces = other_ref.shape[0]
    rows = ROWS
    for k in range(pieces):
        grads[pl.ds(row_of(shard_of(k, 0), rows), rows), :] = near_ref[k * rows : (k + 1) * rows, :]
    for k in range(pieces):
        shard = shard_of(k, 1)
        product = build(ids_ref, shard, other_ref[k], rows)
        base = row_of(shard, rows)
        lanes = product.shape[1]
        for p in range(product.shape[0] // rows):
            grads[pl.ds(base, rows), p * lanes : (p + 1) * lanes] = product[
                p * rows : (p + 1) * rows
            ]

    weight = weight_ref[0:1, 0:1]
    chunk = examples // PARTS
    for c in range(PARTS):
        at = slice(c * chunk, (c + 1) * chunk)
        part = lax.dot_general(grads[...], store_ref[at, :], NT, preferred_element_type=F32)
        placed[:, at] = (part * weight).astype(BF16)

    moved = lax.dot_general(placed[...], choose_ref[...], NT, preferred_element_type=F32)
    moved = moved.astype(BF16)
    for k, pair in ((0, (home, home)), (2, (cross, cross)), (1, (a1, b1)), (3, (a3, b3))):
        for first, out in enumerate(pair):
            for half in range(2):
                row = (k * SIDE + first + 2 * half) * rows
                at = out.shape[0] - (4 - 2 * first) * rows if out.shape[0] > 2 * rows else 0
                at += half * rows
                out[at : at + rows] = moved[row : row + rows]


def scores(ids, near, other, chosen, weight, store):
    queries, examples = ids.shape[0] * ROWS, store.shape[0]
    return pl.pallas_call(
        scores_kernel,
        out_shape=[jax.ShapeDtypeStruct((4 * ROWS, examples), BF16)] * 2
        + [jax.ShapeDtypeStruct((2 * ROWS, examples), BF16)] * 4,
        in_specs=[VMEM] * 6,
        out_specs=[VMEM] * 6,
        scratch_shapes=[
            pltpu.VMEM((queries, store.shape[1]), BF16),
            pltpu.VMEM((queries, examples), BF16),
        ],
        compiler_params=pltpu.CompilerParams(vmem_limit_bytes=8 * MIB),
        name="scores",
    )(ids, near, other, chosen, weight, store)


def add_kernel(first, *refs):
    *parts, a, b = refs
    rows = a.shape[0]
    pieces = [x[...] if x.shape[0] == 2 * rows else x[first : first + 2 * rows] for x in parts]
    one, two, three, four = (x.astype(F32) for x in pieces)
    total = (one + two) + (three + four)
    a[...] = total[:rows].astype(a.dtype)
    b[...] = total[rows:].astype(b.dtype)


def add(first, *parts):
    columns = parts[0].shape[1]
    return pl.pallas_call(
        functools.partial(add_kernel, first),
        out_shape=[jax.ShapeDtypeStruct((ROWS, columns), BF16)] * 2,
        in_specs=[VMEM] * SIDE,
        out_specs=[VMEM] * 2,
        compiler_params=pltpu.CompilerParams(vmem_limit_bytes=4 * MIB),
        name="add",
    )(*parts)


def total_kernel(a, b, c, d, out):
    out[...] = (a[...].astype(F32) + b[...].astype(F32)) + (c[...].astype(F32) + d[...].astype(F32))


def total(*parts):
    return pl.pallas_call(
        total_kernel,
        out_shape=jax.ShapeDtypeStruct(parts[0].shape, F32),
        in_specs=[VMEM] * SIDE,
        out_specs=VMEM,
        compiler_params=pltpu.CompilerParams(vmem_limit_bytes=4 * MIB),
        name="total",
    )(*parts)


def along(parts, axis, shift, order=ORDER):
    n = lax.axis_size(axis)
    return [parts[0]] + [
        lax.ppermute(parts[k], axis, [(i, shift(i, k)) for i in range(n)]) for k in order
    ]


def shards(
    activations,
    cotangents,
    adapter_down,
    projection,
    learning_rates,
    gradient_store,
    example_slot,
    query_of_token,
):
    own = factors(activations[0], cotangents[0], adapter_down[0].T, projection.T)
    near = lax.ppermute(own, "corpus", [(i, i ^ 2) for i in range(16)])
    pair = jnp.stack([own, near])
    chosen, weight, ids = choose(learning_rates, example_slot[0], query_of_token, near)
    mine = jnp.concatenate(
        along([pair] * SIDE, "corpus", lambda i, k: i ^ (4 * k), STEPS[1:])
    )
    mine, chosen = lax.optimization_barrier((mine, chosen))
    other = lax.ppermute(mine, "corpus", [(i, i ^ 1) for i in range(16)])
    store = gradient_store[0]
    near_part = near_grads(ids, mine, store.shape[1])
    home, cross, a1, a3, b1, b3 = scores(ids, near_part, other, chosen, weight, store)
    over_y = lambda x, k: lax.ppermute(x, "ckpt", [(i, i ^ (4 * k)) for i in range(16)])
    over_z = lambda x, k: lax.ppermute(x, "ckpt", [(i, i ^ k) for i in range(16)])
    cross = over_y(cross, 2)
    mine, two = add(0, home, cross, over_y(a1, 1), over_y(a3, 3))
    one, three = add(2 * ROWS, home, cross, over_y(b1, 1), over_y(b3, 3))
    return total(over_z(three, 3), over_z(one, 1), mine, over_z(two, 2))


def solution(mesh):
    return jax.shard_map(
        shards,
        mesh=mesh,
        in_specs=(
            P("ckpt", "corpus", None),
            P("ckpt", "corpus", None),
            P("ckpt", None, None),
            P(),
            P("ckpt"),
            P("ckpt", "corpus", None),
            P("ckpt", "corpus", None),
            P(),
        ),
        out_specs=P("ckpt", "corpus"),
        check_vma=False,
    )
```

```python
import functools

import jax
import jax.numpy as jnp
from jax import lax
from jax.experimental import pallas as pl
from jax.experimental.pallas import tpu as pltpu
from jax.sharding import PartitionSpec as P

BF16 = jnp.bfloat16
F32 = jnp.float32
NT = (((1,), (1,)), ((), ()))
VMEM = pl.BlockSpec(memory_space=pltpu.VMEM)
SMEM = pl.BlockSpec(memory_space=pltpu.SMEM)
HBM = pl.BlockSpec(memory_space=pltpu.HBM)
MIB = 1 << 20
ANY = pl.BlockSpec(memory_space=pl.ANY)
CUTS = 4
PARTS = 2
ROWS = 16
SIDE = 4
ORDER = (2, 1, 3)
STEPS = (0, 1, 3, 2)
PARTED = ((3, 1), (0, 2))


def factors_kernel(act_hbm, cot_hbm, down_hbm, proj_hbm, out_ref, act, cot, down, proj, both, sems):
    pairs = ((act_hbm, act), (down_hbm, down), (cot_hbm, cot), (proj_hbm, proj))
    width = act.shape[1] // CUTS
    copies = [
        [
            pltpu.make_async_copy(
                src.at[:, pl.ds(c * width, width)], dst.at[:, pl.ds(c * width, width)], sems.at[k, c]
            )
            for k, (src, dst) in enumerate(pairs)
        ]
        for c in range(CUTS)
    ]
    for group in copies:
        for copy in group:
            copy.start()
    rank = down.shape[0]
    low_in, low_out = 0.0, 0.0
    for c, group in enumerate(copies):
        for copy in group:
            copy.wait()
        at = slice(c * width, (c + 1) * width)
        low_in += lax.dot_general(down[:, at], act[:, at], NT, preferred_element_type=F32)
        low_out += lax.dot_general(proj[:, at], cot[:, at], NT, preferred_element_type=F32)
    both[...] = low_in
    half = rank // 2
    out_ref[0:half, :] = both[pl.ds(0, half, 2), :].astype(BF16)
    out_ref[half:rank, :] = both[pl.ds(1, half, 2), :].astype(BF16)
    out_ref[rank:, :] = low_out.astype(BF16)


def factors(act, cot, down, proj):
    tokens, rank, width = act.shape[0], down.shape[0], proj.shape[0]
    arrays = [pltpu.with_memory_space_constraint(x, pltpu.HBM) for x in (act, cot, down, proj)]
    return pl.pallas_call(
        factors_kernel,
        out_shape=jax.ShapeDtypeStruct((rank + width, tokens), BF16),
        in_specs=[HBM] * 4,
        out_specs=VMEM,
        scratch_shapes=[pltpu.VMEM(x.shape, BF16) for x in arrays]
        + [pltpu.VMEM((rank, tokens), F32), pltpu.SemaphoreType.DMA((4, CUTS))],
        compiler_params=pltpu.CompilerParams(vmem_limit_bytes=8 * MIB),
        name="factors",
    )(*arrays)


def build(ids_ref, shard, block, rows):
    tokens = block.shape[1]
    half = block.shape[0] // 4
    member = ids_ref[pl.ds(shard, 1), :] == lax.broadcasted_iota(jnp.int32, (rows, tokens), 0)
    low = block[: 2 * half].astype(F32)
    weights = [
        jnp.where(member[None], low[h * half : (h + 1) * half, None, :], 0.0)
        .astype(BF16)
        .reshape(half * rows, tokens)
        for h in range(2)
    ]
    left = jnp.concatenate(weights, axis=1)
    low_out = block[2 * half :]
    blank = jnp.zeros_like(low_out)
    right = jnp.concatenate(
        [
            jnp.concatenate([low_out, blank], axis=1),
            jnp.concatenate([blank, low_out], axis=1),
        ],
        axis=0,
    )
    return lax.dot_general(left, right, NT, preferred_element_type=F32).astype(BF16)


def place(zhi):
    return zhi % 2 * 2 + zhi // 2


def shard_of(k, flip):
    corpus = lax.axis_index("corpus")
    x, zlo, core = corpus // 4, (corpus // 2) % 2, corpus % 2
    return (x ^ STEPS[k // 2]) * 4 + (zlo ^ (k % 2)) * 2 + (core ^ flip)


def row_of(shard, rows):
    ckpt = lax.axis_index("ckpt")
    y, zhi = ckpt // SIDE, ckpt % SIDE
    at = ((shard // SIDE) ^ y) * SIDE + (place(shard % SIDE) + SIDE - place(zhi)) % SIDE
    return pl.multiple_of(at * rows, rows)


def choose_kernel(
    rate_ref, slot_hbm, ids_hbm, after_hbm, out_ref, weight_ref, ids_ref, slot_ref, sems
):
    load = pltpu.make_async_copy(slot_hbm, slot_ref, sems.at[0])
    ids_load = pltpu.make_async_copy(ids_hbm, ids_ref, sems.at[1])
    load.start()
    ids_load.start()
    weight_ref[...] = jnp.full(
        weight_ref.shape, rate_ref[0].astype(F32) * (1.0 / lax.axis_size("ckpt")), F32
    )
    load.wait()
    examples = slot_ref.shape[1]
    slot = slot_ref[...]
    step = 128
    for c in range(examples // step):
        column = lax.broadcasted_iota(jnp.int32, (step, examples), 0) + c * step
        out_ref[c * step : (c + 1) * step, :] = jnp.where(column == slot, 1.0, 0.0).astype(BF16)
    ids_load.wait()


def choose(rate, slot, ids, after):
    examples = slot.shape[1]
    return pl.pallas_call(
        choose_kernel,
        out_shape=[
            jax.ShapeDtypeStruct((examples, examples), BF16),
            jax.ShapeDtypeStruct((8, 128), F32),
            jax.ShapeDtypeStruct(ids.shape, ids.dtype),
        ],
        in_specs=[SMEM, HBM, HBM, ANY],
        out_specs=[VMEM] * 3,
        scratch_shapes=[pltpu.VMEM(slot.shape, jnp.int32), pltpu.SemaphoreType.DMA((2,))],
        compiler_params=pltpu.CompilerParams(vmem_limit_bytes=4 * MIB),
        cost_estimate=pl.CostEstimate(flops=10**10, bytes_accessed=2 * MIB, transcendentals=0),
        name="choose",
    )(rate, *(pltpu.with_memory_space_constraint(x, pltpu.HBM) for x in (slot, ids)), after)


def near_kernel(ids_ref, mine_ref, out_ref):
    rows = out_ref.shape[0] // mine_ref.shape[0]
    for k in range(mine_ref.shape[0]):
        product = build(ids_ref, shard_of(k, 0), mine_ref[k], rows)
        lanes = product.shape[1]
        for p in range(product.shape[0] // rows):
            out_ref[k * rows : (k + 1) * rows, p * lanes : (p + 1) * lanes] = product[
                p * rows : (p + 1) * rows
            ]


def near_grads(ids, mine, width):
    queries = mine.shape[0] * ROWS
    return pl.pallas_call(
        near_kernel,
        out_shape=jax.ShapeDtypeStruct((queries, width), BF16),
        in_specs=[VMEM, VMEM],
        out_specs=VMEM,
        compiler_params=pltpu.CompilerParams(vmem_limit_bytes=4 * MIB),
        cost_estimate=pl.CostEstimate(flops=10**9, bytes_accessed=2 * MIB, transcendentals=0),
        name="near_grads",
    )(ids, mine)


def scores_kernel(
    ids_ref, near_ref, other_ref, choose_ref, weight_ref, store_ref,
    home, cross, a1, a3, b1, b3, grads, placed,
):
    examples = store_ref.shape[0]
    pieces = other_ref.shape[0]
    rows = ROWS
    for k in range(pieces):
        grads[pl.ds(row_of(shard_of(k, 0), rows), rows), :] = near_ref[k * rows : (k + 1) * rows, :]
    for k in range(pieces):
        shard = shard_of(k, 1)
        product = build(ids_ref, shard, other_ref[k], rows)
        base = row_of(shard, rows)
        lanes = product.shape[1]
        for p in range(product.shape[0] // rows):
            grads[pl.ds(base, rows), p * lanes : (p + 1) * lanes] = product[
                p * rows : (p + 1) * rows
            ]

    weight = weight_ref[0:1, 0:1]
    chunk = examples // PARTS
    for c in range(PARTS):
        at = slice(c * chunk, (c + 1) * chunk)
        part = lax.dot_general(grads[...], store_ref[at, :], NT, preferred_element_type=F32)
        placed[:, at] = (part * weight).astype(BF16)

    moved = lax.dot_general(placed[...], choose_ref[...], NT, preferred_element_type=F32)
    moved = moved.astype(BF16)
    for k, pair in ((0, (home, home)), (2, (cross, cross)), (1, (a1, b1)), (3, (a3, b3))):
        for first, out in enumerate(pair):
            for half in range(2):
                row = (k * SIDE + PARTED[first][half]) * rows
                at = out.shape[0] - (4 - 2 * first) * rows if out.shape[0] > 2 * rows else 0
                at += half * rows
                out[at : at + rows] = moved[row : row + rows]


def scores(ids, near, other, chosen, weight, store):
    queries, examples = ids.shape[0] * ROWS, store.shape[0]
    return pl.pallas_call(
        scores_kernel,
        out_shape=[jax.ShapeDtypeStruct((4 * ROWS, examples), BF16)] * 2
        + [jax.ShapeDtypeStruct((2 * ROWS, examples), BF16)] * 4,
        in_specs=[VMEM] * 6,
        out_specs=[VMEM] * 6,
        scratch_shapes=[
            pltpu.VMEM((queries, store.shape[1]), BF16),
            pltpu.VMEM((queries, examples), BF16),
        ],
        compiler_params=pltpu.CompilerParams(vmem_limit_bytes=8 * MIB),
        name="scores",
    )(ids, near, other, chosen, weight, store)


def add_kernel(first, *refs):
    *parts, a, b = refs
    rows = a.shape[0]
    pieces = [x[...] if x.shape[0] == 2 * rows else x[first : first + 2 * rows] for x in parts]
    one, two, three, four = (x.astype(F32) for x in pieces)
    total = (one + two) + (three + four)
    a[...] = total[:rows].astype(a.dtype)
    b[...] = total[rows:].astype(b.dtype)


def add(first, *parts):
    columns = parts[0].shape[1]
    return pl.pallas_call(
        functools.partial(add_kernel, first),
        out_shape=[jax.ShapeDtypeStruct((ROWS, columns), BF16)] * 2,
        in_specs=[VMEM] * SIDE,
        out_specs=[VMEM] * 2,
        compiler_params=pltpu.CompilerParams(vmem_limit_bytes=4 * MIB),
        name="add",
    )(*parts)


def total_kernel(a, b, c, d, out):
    out[...] = (a[...].astype(F32) + b[...].astype(F32)) + (c[...].astype(F32) + d[...].astype(F32))


def total(*parts):
    return pl.pallas_call(
        total_kernel,
        out_shape=jax.ShapeDtypeStruct(parts[0].shape, F32),
        in_specs=[VMEM] * SIDE,
        out_specs=VMEM,
        compiler_params=pltpu.CompilerParams(vmem_limit_bytes=4 * MIB),
        name="total",
    )(*parts)


def along(parts, axis, shift, order=ORDER):
    n = lax.axis_size(axis)
    return [parts[0]] + [
        lax.ppermute(parts[k], axis, [(i, shift(i, k)) for i in range(n)]) for k in order
    ]


def shards(
    activations,
    cotangents,
    adapter_down,
    projection,
    learning_rates,
    gradient_store,
    example_slot,
    query_of_token,
):
    own = factors(activations[0], cotangents[0], adapter_down[0].T, projection.T)
    near = lax.ppermute(own, "corpus", [(i, i ^ 2) for i in range(16)])
    pair = jnp.stack([own, near])
    chosen, weight, ids = choose(learning_rates, example_slot[0], query_of_token, near)
    mine = jnp.concatenate(
        along([pair] * SIDE, "corpus", lambda i, k: i ^ (4 * k), STEPS[1:])
    )
    mine, chosen = lax.optimization_barrier((mine, chosen))
    other = lax.ppermute(mine, "corpus", [(i, i ^ 1) for i in range(16)])
    store = gradient_store[0]
    near_part = near_grads(ids, mine, store.shape[1])
    home, cross, a1, a3, b1, b3 = scores(ids, near_part, other, chosen, weight, store)
    over_y = lambda x, k: lax.ppermute(x, "ckpt", [(i, i ^ (4 * k)) for i in range(16)])

    def over_z(x, step):
        pairs = [(i, i // 4 * 4 + place((place(i % 4) + step) % 4)) for i in range(16)]
        return lax.ppermute(x, "ckpt", pairs)

    cross = over_y(cross, 2)
    three, one = add(0, home, cross, over_y(a1, 1), over_y(a3, 3))
    mine, two = add(2 * ROWS, home, cross, over_y(b1, 1), over_y(b3, 3))
    return total(mine, over_z(two, 2), over_z(three, 3), over_z(one, 1))


def solution(mesh):
    return jax.shard_map(
        shards,
        mesh=mesh,
        in_specs=(
            P("ckpt", "corpus", None),
            P("ckpt", "corpus", None),
            P("ckpt", None, None),
            P(),
            P("ckpt"),
            P("ckpt", "corpus", None),
            P("ckpt", "corpus", None),
            P(),
        ),
        out_specs=P("ckpt", "corpus"),
        check_vma=False,
    )
```

```python
import functools

import jax
import jax.numpy as jnp
from jax import lax
from jax.experimental import pallas as pl
from jax.experimental.pallas import tpu as pltpu
from jax.sharding import PartitionSpec as P

BF16 = jnp.bfloat16
F32 = jnp.float32
NT = (((1,), (1,)), ((), ()))
VMEM = pl.BlockSpec(memory_space=pltpu.VMEM)
SMEM = pl.BlockSpec(memory_space=pltpu.SMEM)
HBM = pl.BlockSpec(memory_space=pltpu.HBM)
MIB = 1 << 20
ANY = pl.BlockSpec(memory_space=pl.ANY)
CUTS = 4
PARTS = 2
ROWS = 16
SIDE = 4
ORDER = (2, 1, 3)
STEPS = (0, 1, 2, 3)
PARTED = ((3, 1), (0, 2))


def factors_kernel(act_hbm, cot_hbm, down_hbm, proj_hbm, out_ref, act, cot, down, proj, both, sems):
    pairs = ((act_hbm, act), (down_hbm, down), (cot_hbm, cot), (proj_hbm, proj))
    width = act.shape[1] // CUTS
    copies = [
        [
            pltpu.make_async_copy(
                src.at[:, pl.ds(c * width, width)], dst.at[:, pl.ds(c * width, width)], sems.at[k, c]
            )
            for k, (src, dst) in enumerate(pairs)
        ]
        for c in range(CUTS)
    ]
    for group in copies:
        for copy in group:
            copy.start()
    rank = down.shape[0]
    low_in, low_out = 0.0, 0.0
    for c, group in enumerate(copies):
        for copy in group:
            copy.wait()
        at = slice(c * width, (c + 1) * width)
        low_in += lax.dot_general(down[:, at], act[:, at], NT, preferred_element_type=F32)
        low_out += lax.dot_general(proj[:, at], cot[:, at], NT, preferred_element_type=F32)
    both[...] = low_in
    half = rank // 2
    out_ref[0:half, :] = both[pl.ds(0, half, 2), :].astype(BF16)
    out_ref[half:rank, :] = both[pl.ds(1, half, 2), :].astype(BF16)
    out_ref[rank:, :] = low_out.astype(BF16)


def factors(act, cot, down, proj):
    tokens, rank, width = act.shape[0], down.shape[0], proj.shape[0]
    arrays = [pltpu.with_memory_space_constraint(x, pltpu.HBM) for x in (act, cot, down, proj)]
    return pl.pallas_call(
        factors_kernel,
        out_shape=jax.ShapeDtypeStruct((rank + width, tokens), BF16),
        in_specs=[HBM] * 4,
        out_specs=VMEM,
        scratch_shapes=[pltpu.VMEM(x.shape, BF16) for x in arrays]
        + [pltpu.VMEM((rank, tokens), F32), pltpu.SemaphoreType.DMA((4, CUTS))],
        compiler_params=pltpu.CompilerParams(vmem_limit_bytes=8 * MIB),
        name="factors",
    )(*arrays)


def build(ids_ref, shard, block, rows):
    tokens = block.shape[1]
    half = block.shape[0] // 4
    member = ids_ref[pl.ds(shard, 1), :] == lax.broadcasted_iota(jnp.int32, (rows, tokens), 0)
    low = block[: 2 * half].astype(F32)
    weights = [
        jnp.where(member[None], low[h * half : (h + 1) * half, None, :], 0.0)
        .astype(BF16)
        .reshape(half * rows, tokens)
        for h in range(2)
    ]
    left = jnp.concatenate(weights, axis=1)
    low_out = block[2 * half :]
    blank = jnp.zeros_like(low_out)
    right = jnp.concatenate(
        [
            jnp.concatenate([low_out, blank], axis=1),
            jnp.concatenate([blank, low_out], axis=1),
        ],
        axis=0,
    )
    return lax.dot_general(left, right, NT, preferred_element_type=F32).astype(BF16)


def place(zhi):
    return zhi % 2 * 2 + zhi // 2


def shard_of(k, flip):
    corpus = lax.axis_index("corpus")
    x, zlo, core = corpus // 4, (corpus // 2) % 2, corpus % 2
    return (x ^ STEPS[k // 2]) * 4 + (zlo ^ (k % 2)) * 2 + (core ^ flip)


def row_of(shard, rows):
    ckpt = lax.axis_index("ckpt")
    y, zhi = ckpt // SIDE, ckpt % SIDE
    at = ((shard // SIDE) ^ y) * SIDE + (place(shard % SIDE) + SIDE - place(zhi)) % SIDE
    return pl.multiple_of(at * rows, rows)


def choose_kernel(
    rate_ref, slot_hbm, ids_hbm, after_hbm, out_ref, weight_ref, ids_ref, slot_ref, sems
):
    load = pltpu.make_async_copy(slot_hbm, slot_ref, sems.at[0])
    ids_load = pltpu.make_async_copy(ids_hbm, ids_ref, sems.at[1])
    load.start()
    ids_load.start()
    weight_ref[...] = jnp.full(
        weight_ref.shape, rate_ref[0].astype(F32) * (1.0 / lax.axis_size("ckpt")), F32
    )
    load.wait()
    examples = slot_ref.shape[1]
    slot = slot_ref[...]
    step = 128
    for c in range(examples // step):
        column = lax.broadcasted_iota(jnp.int32, (step, examples), 0) + c * step
        out_ref[c * step : (c + 1) * step, :] = jnp.where(column == slot, 1.0, 0.0).astype(BF16)
    ids_load.wait()


def choose(rate, slot, ids, after):
    examples = slot.shape[1]
    return pl.pallas_call(
        choose_kernel,
        out_shape=[
            jax.ShapeDtypeStruct((examples, examples), BF16),
            jax.ShapeDtypeStruct((8, 128), F32),
            jax.ShapeDtypeStruct(ids.shape, ids.dtype),
        ],
        in_specs=[SMEM, HBM, HBM, ANY],
        out_specs=[VMEM] * 3,
        scratch_shapes=[pltpu.VMEM(slot.shape, jnp.int32), pltpu.SemaphoreType.DMA((2,))],
        compiler_params=pltpu.CompilerParams(vmem_limit_bytes=4 * MIB),
        cost_estimate=pl.CostEstimate(flops=10**10, bytes_accessed=2 * MIB, transcendentals=0),
        name="choose",
    )(rate, *(pltpu.with_memory_space_constraint(x, pltpu.HBM) for x in (slot, ids)), after)


def near_kernel(ids_ref, mine_ref, out_ref):
    rows = out_ref.shape[0] // mine_ref.shape[0]
    for k in range(mine_ref.shape[0]):
        product = build(ids_ref, shard_of(k, 0), mine_ref[k], rows)
        lanes = product.shape[1]
        for p in range(product.shape[0] // rows):
            out_ref[k * rows : (k + 1) * rows, p * lanes : (p + 1) * lanes] = product[
                p * rows : (p + 1) * rows
            ]


def near_grads(ids, mine, width):
    queries = mine.shape[0] * ROWS
    return pl.pallas_call(
        near_kernel,
        out_shape=jax.ShapeDtypeStruct((queries, width), BF16),
        in_specs=[VMEM, VMEM],
        out_specs=VMEM,
        compiler_params=pltpu.CompilerParams(vmem_limit_bytes=4 * MIB),
        cost_estimate=pl.CostEstimate(flops=10**9, bytes_accessed=2 * MIB, transcendentals=0),
        name="near_grads",
    )(ids, mine)


def scores_kernel(
    ids_ref, near_ref, other_ref, choose_ref, weight_ref, store_ref,
    home, cross, a1, a3, b1, b3, grads, placed,
):
    examples = store_ref.shape[0]
    pieces = other_ref.shape[0]
    rows = ROWS
    for k in range(pieces):
        grads[pl.ds(row_of(shard_of(k, 0), rows), rows), :] = near_ref[k * rows : (k + 1) * rows, :]
    for k in range(pieces):
        shard = shard_of(k, 1)
        product = build(ids_ref, shard, other_ref[k], rows)
        base = row_of(shard, rows)
        lanes = product.shape[1]
        for p in range(product.shape[0] // rows):
            grads[pl.ds(base, rows), p * lanes : (p + 1) * lanes] = product[
                p * rows : (p + 1) * rows
            ]

    weight = weight_ref[0:1, 0:1]
    chunk = examples // PARTS
    for c in range(PARTS):
        at = slice(c * chunk, (c + 1) * chunk)
        part = lax.dot_general(grads[...], store_ref[at, :], NT, preferred_element_type=F32)
        placed[:, at] = (part * weight).astype(BF16)

    moved = lax.dot_general(placed[...], choose_ref[...], NT, preferred_element_type=F32)
    for k, pair in ((0, (home, home)), (3, (cross, cross)), (2, (a1, b1)), (1, (a3, b3))):
        for first, out in enumerate(pair):
            for half in range(2):
                row = (k * SIDE + PARTED[first][half]) * rows
                at = out.shape[0] - (4 - 2 * first) * rows if out.shape[0] > 2 * rows else 0
                at += half * rows
                out[at : at + rows] = moved[row : row + rows].astype(out.dtype)


def scores(ids, near, other, chosen, weight, store):
    queries, examples = ids.shape[0] * ROWS, store.shape[0]
    return pl.pallas_call(
        scores_kernel,
        out_shape=[jax.ShapeDtypeStruct((4 * ROWS, examples), BF16)] * 2
        + [jax.ShapeDtypeStruct((2 * ROWS, examples), BF16)] * 4,
        in_specs=[VMEM] * 6,
        out_specs=[VMEM] * 6,
        scratch_shapes=[
            pltpu.VMEM((queries, store.shape[1]), BF16),
            pltpu.VMEM((queries, examples), BF16),
        ],
        compiler_params=pltpu.CompilerParams(vmem_limit_bytes=8 * MIB),
        name="scores",
    )(ids, near, other, chosen, weight, store)


def add_kernel(first, *refs):
    *parts, a, b = refs
    rows = a.shape[0]
    pieces = [x[...] if x.shape[0] == 2 * rows else x[first : first + 2 * rows] for x in parts]
    one, two, three, four = (x.astype(F32) for x in pieces)
    total = (one + two) + (three + four)
    a[...] = total[:rows].astype(a.dtype)
    b[...] = total[rows:].astype(b.dtype)


def add(first, *parts):
    columns = parts[0].shape[1]
    return pl.pallas_call(
        functools.partial(add_kernel, first),
        out_shape=[jax.ShapeDtypeStruct((ROWS, columns), F32 if first else BF16)]
        + [jax.ShapeDtypeStruct((ROWS, columns), BF16)],
        in_specs=[VMEM] * SIDE,
        out_specs=[VMEM] * 2,
        compiler_params=pltpu.CompilerParams(vmem_limit_bytes=4 * MIB),
        name="add",
    )(*parts)


def total_kernel(a, b, c, d, out):
    out[...] = (a[...].astype(F32) + b[...].astype(F32)) + (c[...].astype(F32) + d[...].astype(F32))


def total(*parts):
    return pl.pallas_call(
        total_kernel,
        out_shape=jax.ShapeDtypeStruct(parts[0].shape, F32),
        in_specs=[VMEM] * SIDE,
        out_specs=VMEM,
        compiler_params=pltpu.CompilerParams(vmem_limit_bytes=4 * MIB),
        name="total",
    )(*parts)


def along(parts, axis, shift, order=ORDER):
    n = lax.axis_size(axis)
    return [parts[0]] + [
        lax.ppermute(parts[k], axis, [(i, shift(i, k)) for i in range(n)]) for k in order
    ]


def shards(
    activations,
    cotangents,
    adapter_down,
    projection,
    learning_rates,
    gradient_store,
    example_slot,
    query_of_token,
):
    own = factors(activations[0], cotangents[0], adapter_down[0].T, projection.T)
    near = lax.ppermute(own, "corpus", [(i, i ^ 2) for i in range(16)])
    pair = jnp.stack([own, near])
    chosen, weight, ids = choose(learning_rates, example_slot[0], query_of_token, near)
    mine = jnp.concatenate(
        along([pair] * SIDE, "corpus", lambda i, k: i ^ (4 * k), STEPS[1:])
    )
    mine, chosen = lax.optimization_barrier((mine, chosen))
    other = lax.ppermute(mine, "corpus", [(i, i ^ 1) for i in range(16)])
    store = gradient_store[0]
    near_part = near_grads(ids, mine, store.shape[1])
    home, cross, a1, a3, b1, b3 = scores(ids, near_part, other, chosen, weight, store)
    over_y = lambda x, k: lax.ppermute(x, "ckpt", [(i, i ^ (4 * k)) for i in range(16)])

    def over_z(x, step):
        pairs = [(i, i // 4 * 4 + place((place(i % 4) + step) % 4)) for i in range(16)]
        return lax.ppermute(x, "ckpt", pairs)

    cross = over_y(cross, 3)
    three, one = add(0, home, cross, over_y(a1, 2), over_y(a3, 1))
    mine, two = add(2 * ROWS, home, cross, over_y(b1, 2), over_y(b3, 1))
    return total(mine, over_z(two, 2), over_z(three, 3), over_z(one, 1))


def solution(mesh):
    return jax.shard_map(
        shards,
        mesh=mesh,
        in_specs=(
            P("ckpt", "corpus", None),
            P("ckpt", "corpus", None),
            P("ckpt", None, None),
            P(),
            P("ckpt"),
            P("ckpt", "corpus", None),
            P("ckpt", "corpus", None),
            P(),
        ),
        out_specs=P("ckpt", "corpus"),
        check_vma=False,
    )
```

```python
import functools

import jax
import jax.numpy as jnp
from jax import lax
from jax.experimental import pallas as pl
from jax.experimental.pallas import tpu as pltpu
from jax.sharding import PartitionSpec as P

BF16 = jnp.bfloat16
F32 = jnp.float32
NT = (((1,), (1,)), ((), ()))
VMEM = pl.BlockSpec(memory_space=pltpu.VMEM)
SMEM = pl.BlockSpec(memory_space=pltpu.SMEM)
HBM = pl.BlockSpec(memory_space=pltpu.HBM)
MIB = 1 << 20
ANY = pl.BlockSpec(memory_space=pl.ANY)
CUTS = 4
PARTS = 2
ROWS = 16
SIDE = 4
ORDER = (2, 1, 3)
STEPS = (0, 1, 2, 3)
PARTED = ((3, 1), (0, 2))


def factors_kernel(act_hbm, cot_hbm, down_hbm, proj_hbm, out_ref, act, cot, down, proj, both, sems):
    pairs = ((act_hbm, act), (down_hbm, down), (cot_hbm, cot), (proj_hbm, proj))
    width = act.shape[1] // CUTS
    copies = [
        [
            pltpu.make_async_copy(
                src.at[:, pl.ds(c * width, width)], dst.at[:, pl.ds(c * width, width)], sems.at[k, c]
            )
            for k, (src, dst) in enumerate(pairs)
        ]
        for c in range(CUTS)
    ]
    for group in copies:
        for copy in group:
            copy.start()
    rank = down.shape[0]
    low_in, low_out = 0.0, 0.0
    for c, group in enumerate(copies):
        for copy in group:
            copy.wait()
        at = slice(c * width, (c + 1) * width)
        low_in += lax.dot_general(down[:, at], act[:, at], NT, preferred_element_type=F32)
        low_out += lax.dot_general(proj[:, at], cot[:, at], NT, preferred_element_type=F32)
    both[...] = low_in
    half = rank // 2
    out_ref[0:half, :] = both[pl.ds(0, half, 2), :].astype(BF16)
    out_ref[half:rank, :] = both[pl.ds(1, half, 2), :].astype(BF16)
    out_ref[rank:, :] = low_out.astype(BF16)


def factors(act, cot, down, proj):
    tokens, rank, width = act.shape[0], down.shape[0], proj.shape[0]
    arrays = [pltpu.with_memory_space_constraint(x, pltpu.HBM) for x in (act, cot, down, proj)]
    return pl.pallas_call(
        factors_kernel,
        out_shape=jax.ShapeDtypeStruct((rank + width, tokens), BF16),
        in_specs=[HBM] * 4,
        out_specs=VMEM,
        scratch_shapes=[pltpu.VMEM(x.shape, BF16) for x in arrays]
        + [pltpu.VMEM((rank, tokens), F32), pltpu.SemaphoreType.DMA((4, CUTS))],
        compiler_params=pltpu.CompilerParams(vmem_limit_bytes=8 * MIB),
        name="factors",
    )(*arrays)


def build(ids_ref, shard, block, rows):
    tokens = block.shape[1]
    half = block.shape[0] // 4
    member = ids_ref[pl.ds(shard, 1), :] == lax.broadcasted_iota(jnp.int32, (rows, tokens), 0)
    low = block[: 2 * half].astype(F32)
    weights = [
        jnp.where(member[None], low[h * half : (h + 1) * half, None, :], 0.0)
        .astype(BF16)
        .reshape(half * rows, tokens)
        for h in range(2)
    ]
    left = jnp.concatenate(weights, axis=1)
    low_out = block[2 * half :]
    blank = jnp.zeros_like(low_out)
    right = jnp.concatenate(
        [
            jnp.concatenate([low_out, blank], axis=1),
            jnp.concatenate([blank, low_out], axis=1),
        ],
        axis=0,
    )
    return lax.dot_general(left, right, NT, preferred_element_type=F32).astype(BF16)


def place(zhi):
    return zhi % 2 * 2 + zhi // 2


def shard_of(k, flip):
    corpus = lax.axis_index("corpus")
    x, zlo, core = corpus // 4, (corpus // 2) % 2, corpus % 2
    return (x ^ STEPS[k // 2]) * 4 + (zlo ^ (k % 2)) * 2 + (core ^ flip)


def row_of(shard, rows):
    ckpt = lax.axis_index("ckpt")
    y, zhi = ckpt // SIDE, ckpt % SIDE
    at = ((shard // SIDE) ^ y) * SIDE + (place(shard % SIDE) + SIDE - place(zhi)) % SIDE
    return pl.multiple_of(at * rows, rows)


def choose_kernel(
    rate_ref, slot_hbm, ids_hbm, after_hbm, out_ref, weight_ref, ids_ref, slot_ref, sems
):
    load = pltpu.make_async_copy(slot_hbm, slot_ref, sems.at[0])
    ids_load = pltpu.make_async_copy(ids_hbm, ids_ref, sems.at[1])
    load.start()
    ids_load.start()
    weight_ref[...] = jnp.full(
        weight_ref.shape, rate_ref[0].astype(F32) * (1.0 / lax.axis_size("ckpt")), F32
    )
    load.wait()
    examples = slot_ref.shape[1]
    slot = slot_ref[...]
    step = 128
    for c in range(examples // step):
        column = lax.broadcasted_iota(jnp.int32, (step, examples), 0) + c * step
        out_ref[c * step : (c + 1) * step, :] = jnp.where(column == slot, 1.0, 0.0).astype(BF16)
    ids_load.wait()


def choose(rate, slot, ids, after):
    examples = slot.shape[1]
    return pl.pallas_call(
        choose_kernel,
        out_shape=[
            jax.ShapeDtypeStruct((examples, examples), BF16),
            jax.ShapeDtypeStruct((8, 128), F32),
            jax.ShapeDtypeStruct(ids.shape, ids.dtype),
        ],
        in_specs=[SMEM, HBM, HBM, ANY],
        out_specs=[VMEM] * 3,
        scratch_shapes=[pltpu.VMEM(slot.shape, jnp.int32), pltpu.SemaphoreType.DMA((2,))],
        compiler_params=pltpu.CompilerParams(vmem_limit_bytes=4 * MIB),
        cost_estimate=pl.CostEstimate(flops=10**10, bytes_accessed=2 * MIB, transcendentals=0),
        name="choose",
    )(rate, *(pltpu.with_memory_space_constraint(x, pltpu.HBM) for x in (slot, ids)), after)


def near_kernel(ids_ref, mine_ref, out_ref):
    rows = out_ref.shape[0] // mine_ref.shape[0]
    for k in range(mine_ref.shape[0]):
        product = build(ids_ref, shard_of(k, 0), mine_ref[k], rows)
        lanes = product.shape[1]
        for p in range(product.shape[0] // rows):
            out_ref[k * rows : (k + 1) * rows, p * lanes : (p + 1) * lanes] = product[
                p * rows : (p + 1) * rows
            ]


def near_grads(ids, mine, width):
    queries = mine.shape[0] * ROWS
    return pl.pallas_call(
        near_kernel,
        out_shape=jax.ShapeDtypeStruct((queries, width), BF16),
        in_specs=[VMEM, VMEM],
        out_specs=VMEM,
        compiler_params=pltpu.CompilerParams(vmem_limit_bytes=4 * MIB),
        cost_estimate=pl.CostEstimate(flops=10**9, bytes_accessed=2 * MIB, transcendentals=0),
        name="near_grads",
    )(ids, mine)


def scores_kernel(
    ids_ref, near_ref, other_ref, choose_ref, weight_ref, store_ref,
    home, cross, a1, a3, b1, b3, grads, placed,
):
    examples = store_ref.shape[0]
    pieces = other_ref.shape[0]
    rows = ROWS
    for k in range(pieces):
        grads[pl.ds(row_of(shard_of(k, 0), rows), rows), :] = near_ref[k * rows : (k + 1) * rows, :]
    for k in range(pieces):
        shard = shard_of(k, 1)
        product = build(ids_ref, shard, other_ref[k], rows)
        base = row_of(shard, rows)
        lanes = product.shape[1]
        for p in range(product.shape[0] // rows):
            grads[pl.ds(base, rows), p * lanes : (p + 1) * lanes] = product[
                p * rows : (p + 1) * rows
            ]

    weight = weight_ref[0:1, 0:1]
    chunk = examples // PARTS
    for c in range(PARTS):
        at = slice(c * chunk, (c + 1) * chunk)
        part = lax.dot_general(grads[...], store_ref[at, :], NT, preferred_element_type=F32)
        placed[:, at] = (part * weight).astype(BF16)

    moved = lax.dot_general(placed[...], choose_ref[...], NT, preferred_element_type=F32)
    for k, pair in ((0, (home, home)), (3, (cross, cross)), (2, (a1, b1)), (1, (a3, b3))):
        for first, out in enumerate(pair):
            for half in range(2):
                row = (k * SIDE + PARTED[first][half]) * rows
                at = out.shape[0] - (4 - 2 * first) * rows if out.shape[0] > 2 * rows else 0
                at += half * rows
                out[at : at + rows] = moved[row : row + rows].astype(out.dtype)


def scores(ids, near, other, chosen, weight, store):
    queries, examples = ids.shape[0] * ROWS, store.shape[0]
    return pl.pallas_call(
        scores_kernel,
        out_shape=[jax.ShapeDtypeStruct((4 * ROWS, examples), BF16)] * 2
        + [jax.ShapeDtypeStruct((2 * ROWS, examples), BF16)] * 4,
        in_specs=[VMEM] * 6,
        out_specs=[VMEM] * 6,
        scratch_shapes=[
            pltpu.VMEM((queries, store.shape[1]), BF16),
            pltpu.VMEM((queries, examples), BF16),
        ],
        compiler_params=pltpu.CompilerParams(vmem_limit_bytes=8 * MIB),
        name="scores",
    )(ids, near, other, chosen, weight, store)


def add_kernel(first, *refs):
    *parts, a, b = refs
    rows = a.shape[0]
    pieces = [x[...] if x.shape[0] == 2 * rows else x[first : first + 2 * rows] for x in parts]
    one, two, three, four = (x.astype(F32) for x in pieces)
    total = (one + two) + (three + four)
    a[...] = total[:rows].astype(a.dtype)
    b[...] = total[rows:].astype(b.dtype)


def add(first, *parts):
    columns = parts[0].shape[1]
    return pl.pallas_call(
        functools.partial(add_kernel, first),
        out_shape=[jax.ShapeDtypeStruct((ROWS, columns), F32 if first else BF16)]
        + [jax.ShapeDtypeStruct((ROWS, columns), BF16)],
        in_specs=[VMEM] * SIDE,
        out_specs=[VMEM] * 2,
        compiler_params=pltpu.CompilerParams(vmem_limit_bytes=4 * MIB),
        name="add",
    )(*parts)


def total_kernel(a, b, c, d, out):
    out[...] = (a[...].astype(F32) + b[...].astype(F32)) + (c[...].astype(F32) + d[...].astype(F32))


def total(*parts):
    return pl.pallas_call(
        total_kernel,
        out_shape=jax.ShapeDtypeStruct(parts[0].shape, F32),
        in_specs=[VMEM] * SIDE,
        out_specs=VMEM,
        compiler_params=pltpu.CompilerParams(vmem_limit_bytes=4 * MIB),
        name="total",
    )(*parts)


def along(parts, axis, shift, order=ORDER):
    n = lax.axis_size(axis)
    return [parts[0]] + [
        lax.ppermute(parts[k], axis, [(i, shift(i, k)) for i in range(n)]) for k in order
    ]


def shards(
    activations,
    cotangents,
    adapter_down,
    projection,
    learning_rates,
    gradient_store,
    example_slot,
    query_of_token,
):
    own = factors(activations[0], cotangents[0], adapter_down[0].T, projection.T)
    near = lax.ppermute(own, "corpus", [(i, i ^ 2) for i in range(16)])
    pair = jnp.stack([own, near])
    chosen, weight, ids = choose(learning_rates, example_slot[0], query_of_token, near)
    mine = jnp.concatenate(
        along([pair] * SIDE, "corpus", lambda i, k: i ^ (4 * k), STEPS[1:])
    )
    mine, chosen = lax.optimization_barrier((mine, chosen))
    other = lax.ppermute(mine, "corpus", [(i, i ^ 1) for i in range(16)])
    store = gradient_store[0]
    near_part = near_grads(ids, mine, store.shape[1])
    home, cross, a1, a3, b1, b3 = scores(ids, near_part, other, chosen, weight, store)
    over_y = lambda x, k: lax.ppermute(x, "ckpt", [(i, i ^ (4 * k)) for i in range(16)])

    def over_z(x, step):
        pairs = [(i, i // 4 * 4 + place((place(i % 4) + step) % 4)) for i in range(16)]
        return lax.ppermute(x, "ckpt", pairs)

    cross = over_y(cross, 3)
    three, one = add(0, home, cross, over_y(a1, 2), over_y(a3, 1))
    mine, two = add(2 * ROWS, home, cross, over_y(b3, 1), over_y(b1, 2))
    return total(mine, over_z(two, 2), over_z(three, 3), over_z(one, 1))


def solution(mesh):
    return jax.shard_map(
        shards,
        mesh=mesh,
        in_specs=(
            P("ckpt", "corpus", None),
            P("ckpt", "corpus", None),
            P("ckpt", None, None),
            P(),
            P("ckpt"),
            P("ckpt", "corpus", None),
            P("ckpt", "corpus", None),
            P(),
        ),
        out_specs=P("ckpt", "corpus"),
        check_vma=False,
    )
```
